512 devices in a mesh: gx: 32 (over y, x_hi, core), gz: 16 (over z, x_lo).
Axes of the slice: x: 4 (x_hi: 2, x_lo: 2; x = x_hi * 2 + x_lo), y: 8, z: 8, core: 2. Of those that a mesh axis runs over, the one named last changes fastest.
Arguments:
- multipoles: float32 [81, 64, 32, 2048], P(None, 'gx', None, 'gz')
- kernel_base: float32 [81, 81], replicated, may hold values from -0.625 to 0.625
- kernel_freq: float32 [1025, 81], replicated, may hold values from 0.25 to 2
- res_off: bfloat16 [32, 16, 32, 3, 128], P('gx', 'gz'), may hold values from -0.5 to 0.5
- res_count: int32 [32, 16, 32], P('gx', 'gz'), may hold values from 32 to 128, as said below
- res_scale: float32 [32, 16, 32], P('gx', 'gz'), may hold values from 0.5 to 1
- leave_off: bfloat16 [32, 16, 16, 3, 128], P('gx', 'gz'), may hold values from -0.5 to 0.5
- leave_count: int32 [32, 16, 16], P('gx', 'gz'), may hold values from 32 to 128, as said below
- leave_dest: int32 [32, 16, 16], P('gx', 'gz'), may hold values from 0 to 31
- leave_scale: float32 [32, 16, 16], P('gx', 'gz'), may hold values from 0.5 to 1
- route_blocks: int32 [32, 16, 2, 8], P('gx', 'gz'), may hold values from 0 to 15, as said below
- route_num: int32 [32, 16, 2], P('gx', 'gz'), may hold values from 1 to 8
Outputs:
- taylors: float32 [81, 64, 32, 2048], P(None, 'gx', None, 'gz')
- near_accel: float32 [32, 16, 32, 3, 128], P('gx', 'gz')
The draws below stay inside these ranges and needn't reach their ends.
Inputs may be any that keep to these rules, and one draw needn't show every extreme that they name: `res_count`: live particles of a block fill its first slots. `leave_count`: live particles of a block fill its first slots. `route_blocks`: row 0 lists the device's leaving blocks bound for the slab at the next lower gx index, row 1 those for the next higher (periodically); the two rows of a device name distinct blocks of its pool; only the first route_num entries of a row are used.
All inputs are finite; a program needn't handle non-finite values.
Results may differ from the reference program's by a relative error of at most 0.0003.
Values may be sent and summed in bfloat16 or wider, within the bound.
A program may use at most 128 MiB of HBM per device.

```python
import math
from functools import partial
import jax
import jax.numpy as jnp
from jax import lax

COMPS = 81
NZ = 2048
NY = 32
BLK = 32
MAXB = 8
SLOT = 128
POOL = 16
NX = 64
HALF = 1025
N_GX = 32
N_GZ = 16


def block_counts(key, shape):
    first_key, second_key = jax.random.split(key)
    missing = jax.random.randint(first_key, shape, 0, SLOT * 3 // 4 + 1)
    filled = jax.random.randint(second_key, shape, 0, 3) == 0
    return jnp.where(filled, SLOT, SLOT - missing).astype(jnp.int32)


def draw_multipoles(key, part):
    key = jax.random.fold_in(key, 11)
    shape = (COMPS, NX, NY, NZ)
    return jax.random.normal(key, shape, jnp.float32)


def draw_res_count(key, part):
    key = jax.random.fold_in(key, 3)
    return block_counts(key, (N_GX, N_GZ, BLK))


def draw_leave_count(key, part):
    key = jax.random.fold_in(key, 5)
    return block_counts(key, (N_GX, N_GZ, POOL))


def draw_route_blocks(key, part):
    key = jax.random.fold_in(key, 23)
    device_keys = jax.random.split(key, N_GX * N_GZ)
    orders = jax.vmap(lambda device_key: jax.random.permutation(device_key, POOL))(device_keys)
    return orders.reshape(N_GX, N_GZ, 2, MAXB).astype(jnp.int32)


def draw_route_num(key, part):
    key = jax.random.fold_in(key, 37)
    first_key, second_key = jax.random.split(key)
    total = N_GX * N_GZ * 2
    counts = jax.random.randint(first_key, (total,), 1, MAXB + 1)
    chosen = jax.random.randint(second_key, (), 0, total)
    counts = jnp.where(jnp.arange(total, dtype=jnp.int32) == chosen, MAXB, counts)
    return counts.reshape(N_GX, N_GZ, 2).astype(jnp.int32)


def touch_ends(values, own_key, low, largest):
    longest = values.shape.index(max(values.shape))
    spots = []
    for shift in (0, 1):
        where = [jax.random.randint(jax.random.fold_in(own_key, axis), (), 0, length) for axis, length in enumerate(values.shape)]
        where[longest] = (where[longest] + shift) % values.shape[longest]
        spots.append(tuple(where))
    return values.at[spots[0]].set(low).at[spots[1]].set(largest)


def shard_levels(own_key, extent, cuts, smallest, top_value):
    factor_of, own = 1.0, jax.random.fold_in(own_key, 6)
    for dim, shards_of in cuts:
        steps = jnp.exp(jax.random.uniform(jax.random.fold_in(own, dim), (shards_of,), jnp.float32, smallest / len(cuts), top_value / len(cuts)))
        factor_of = factor_of * jnp.repeat(steps, extent[dim] // shards_of).reshape([-1 if axis == dim else 1 for axis in range(len(extent))])
    return factor_of


def bell_draw(stream_key, shape, deviation, limit, held_as=jnp.bfloat16):
    values = jax.random.normal(stream_key, shape, jnp.float32) * deviation
    return jnp.minimum(jnp.maximum(values, -limit), limit).astype(held_as)


def setup_inputs(seed: int = 0) -> dict:
    key_list = jax.random.split(jax.random.key(seed), 13)
    multipoles = draw_multipoles(jax.random.fold_in(key_list[12], 71), 0)
    kernel_base = bell_draw(key_list[1], (COMPS, COMPS), COMPS ** -0.5, 0.625, jnp.float32)
    kernel_freq = jnp.clip(jax.random.uniform(key_list[2], (HALF, COMPS), jnp.float32, 0.25, 2.0), 0.25, 2.0)
    res_off = jnp.clip(jax.random.uniform(key_list[3], (N_GX, N_GZ, BLK, 3, SLOT), jnp.float32, -0.5, 0.5) * shard_levels(key_list[3], (N_GX, N_GZ, BLK, 3, SLOT), ((0, 32), (1, 16)), -0.4, 0.0), -0.5, 0.5).astype(jnp.bfloat16)
    res_count = draw_res_count(jax.random.fold_in(key_list[12], 71), 0)
    res_scale = jnp.clip(jnp.exp(math.log(1.0) - 0.6931472 * jax.random.uniform(key_list[5], (N_GX, N_GZ, BLK), jnp.float32) ** shard_levels(key_list[5], (N_GX, N_GZ, BLK), ((0, 32), (1, 16)), -0.2, 0.2)), 0.5, 1.0)
    leave_off = jnp.clip(jax.random.uniform(key_list[6], (N_GX, N_GZ, POOL, 3, SLOT), jnp.float32, -0.5, 0.5) * shard_levels(key_list[6], (N_GX, N_GZ, POOL, 3, SLOT), ((0, 32), (1, 16)), -0.4, 0.0), -0.5, 0.5).astype(jnp.bfloat16)
    leave_count = draw_leave_count(jax.random.fold_in(key_list[12], 71), 0)
    leave_dest = touch_ends(jax.random.randint(key_list[8], (N_GX, N_GZ, POOL), 0, BLK), jax.random.fold_in(key_list[8], 1), 0, BLK - 1).astype(jnp.int32)
    leave_scale = jnp.clip(jnp.exp(math.log(1.0) - 0.6931472 * jax.random.uniform(key_list[9], (N_GX, N_GZ, POOL), jnp.float32) ** shard_levels(key_list[9], (N_GX, N_GZ, POOL), ((0, 32), (1, 16)), -0.2, 0.2)), 0.5, 1.0)
    route_blocks = draw_route_blocks(jax.random.fold_in(key_list[12], 71), 0)
    route_num = draw_route_num(jax.random.fold_in(key_list[12], 71), 0)
    return {"multipoles": multipoles, "kernel_base": kernel_base, "kernel_freq": kernel_freq, "res_off": res_off, "res_count": res_count, "res_scale": res_scale, "leave_off": leave_off, "leave_count": leave_count, "leave_dest": leave_dest, "leave_scale": leave_scale, "route_blocks": route_blocks, "route_num": route_num}


highest = lax.Precision.HIGHEST
softening_sq = 0.04
particle_mass = 1.0 / 128.0

def pair_accel(sink_pos, sources, masses):
    separation = sources[:, :, :, None] - sink_pos[:, :, None, :]
    distance = lax.optimization_barrier(jnp.sum(separation * separation, axis=1)) + softening_sq
    inverse = lax.rsqrt(distance)
    weight = masses[:, :, None] * inverse * inverse * inverse
    return lax.optimization_barrier(jnp.sum(separation * weight[:, None, :, :], axis=2))

def near_field(res_pos, res_mass, arrivals):
    blocks, dims, slots = res_pos.shape
    pad_pos = jnp.pad(res_pos, ((1, 1), (0, 0), (0, 0)))
    pad_mass = jnp.pad(res_mass, ((1, 1), (0, 0)))
    src_pos = jnp.concatenate([pad_pos[0:blocks], pad_pos[1:blocks + 1], pad_pos[2:blocks + 2]], axis=2)
    src_mass = jnp.concatenate([pad_mass[0:blocks], pad_mass[1:blocks + 1], pad_mass[2:blocks + 2]], axis=1)
    groups = blocks // 8

    def group_accel(members):
        return pair_accel(members[0], members[1], members[2])
    resident = lax.map(group_accel, (res_pos.reshape(groups, 8, dims, slots), src_pos.reshape(groups, 8, dims, 3 * slots), src_mass.reshape(groups, 8, 3 * slots)))
    resident = resident.reshape(blocks, dims, slots)
    targets = arrivals[:, 4, 0].astype(jnp.int32)
    target_f = targets.astype(res_pos.dtype)
    zero_col = jnp.zeros_like(target_f)
    centres = jnp.stack([zero_col, target_f, zero_col], axis=1)
    arr_pos = arrivals[:, 0:3, :].astype(res_pos.dtype) + centres[:, :, None]
    arr_mass = arrivals[:, 3, :].astype(res_pos.dtype)
    sink_pos = res_pos[targets]
    incoming = pair_accel(sink_pos, arr_pos, arr_mass)
    onehot = (targets[:, None] == jnp.arange(blocks, dtype=jnp.int32)[None, :]).astype(res_pos.dtype)
    return resident + jnp.einsum('ab,acs->bcs', onehot, incoming, precision=highest)

def slab_taylors(kernel_base, kernel_freq, slab):
    spectrum = jnp.fft.rfft(slab, axis=2)
    gain = jnp.transpose(kernel_freq)[:, None, :]
    mixed_re = jnp.einsum('jk,kyf->jyf', kernel_base, jnp.real(spectrum) * gain, precision=highest)
    mixed_im = jnp.einsum('jk,kyf->jyf', kernel_base, jnp.imag(spectrum) * gain, precision=highest)
    return jnp.fft.irfft(mixed_re + 1j * mixed_im, n=NZ, axis=2).astype(slab.dtype)

def reference(multipoles, kernel_base, kernel_freq, res_off, res_count, res_scale, leave_off, leave_count, leave_dest, leave_scale, route_blocks, route_num):
    moved = lax.map(partial(slab_taylors, kernel_base, kernel_freq), jnp.moveaxis(multipoles, 1, 0))
    taylors = jnp.moveaxis(moved, 0, 1)
    slot_ids = jnp.arange(SLOT, dtype=jnp.int32)
    block_f = jnp.arange(BLK, dtype=jnp.int32).astype(res_scale.dtype)
    zero_col = jnp.zeros_like(block_f)
    centres = jnp.stack([zero_col, block_f, zero_col], axis=1)
    res_pos = res_scale[..., None, None] * res_off.astype(res_scale.dtype) + centres[None, None, :, :, None]
    res_mass = jnp.where(slot_ids < res_count[..., None], jnp.float32(particle_mass), jnp.float32(0.0))
    block_ids = route_blocks.reshape(N_GX, N_GZ, 2 * MAXB)
    index_full = jnp.broadcast_to(block_ids[..., None, None], (N_GX, N_GZ, 2 * MAXB, 3, SLOT))
    offsets = jnp.take_along_axis(leave_off, index_full, axis=2)
    scales = jnp.take_along_axis(leave_scale, block_ids, axis=2)
    counts = jnp.take_along_axis(leave_count, block_ids, axis=2)
    targets = jnp.take_along_axis(leave_dest, block_ids, axis=2)
    in_use = (jnp.arange(MAXB, dtype=jnp.int32)[None, None, None, :] < route_num[..., None]).reshape(N_GX, N_GZ, 2 * MAXB)
    scaled = (scales[..., None, None] * offsets.astype(scales.dtype)).astype(jnp.bfloat16)
    live = in_use[..., None] & (slot_ids < counts[..., None])
    mass_row = jnp.where(live, jnp.float32(particle_mass), jnp.float32(0.0)).astype(jnp.bfloat16)[..., None, :]
    target_row = jnp.broadcast_to(targets.astype(jnp.bfloat16)[..., None, None], (N_GX, N_GZ, 2 * MAXB, 1, SLOT))
    packed = jnp.concatenate([scaled, mass_row, target_row], axis=3).reshape(N_GX, N_GZ, 2, MAXB, 5, SLOT)
    arrivals = jnp.concatenate([jnp.roll(packed[:, :, 1], 1, axis=0), jnp.roll(packed[:, :, 0], -1, axis=0)], axis=2)
    devices = N_GX * N_GZ

    def device_near(members):
        return near_field(members[0], members[1], members[2])
    near_accel = lax.map(device_near, (res_pos.reshape(devices, BLK, 3, SLOT), res_mass.reshape(devices, BLK, SLOT), arrivals.reshape(devices, 2 * MAXB, 5, SLOT)))
    return (taylors, near_accel.reshape(N_GX, N_GZ, BLK, 3, SLOT))
```

```python
import math

import jax
import jax.numpy as jnp
import numpy as np
from jax import lax
from jax.experimental import pallas as pl
from jax.experimental.pallas import tpu as pltpu
from jax.sharding import PartitionSpec as P

softening_sq = 0.04
particle_mass = 1.0 / 128.0
MESH = pl.DeviceIdType.MESH

COMPS = 81
ROWS = 88
SENT = 82
GZ = 16
GX = 32
PLANES = 128
CELLS = 64
HALVES = 9
BLK = 32
POOL = 16
MAXB = 8
TOP = 32700.0
CODE = 128.0
ROOT = math.sqrt(TOP)


def dft_tables():
    r = np.arange(PLANES)
    j = np.arange(PLANES)
    f2 = np.where(j < 64, j, 191 - j)
    angle = 2.0 * np.pi * ((r[:, None] * f2[None, :]) % PLANES) / PLANES
    c, s = np.cos(angle), np.sin(angle)
    forward = np.block([[c, -s], [s, c]])
    inverse = np.block([[c.T, s.T], [-s.T, c.T]])
    turn = 2.0 * np.pi * np.arange(HALVES)[:, None] * r[None, :] / (GZ * PLANES)
    twiddle = np.zeros((2, 16, PLANES))
    twiddle[0, :HALVES] = np.cos(turn)
    twiddle[1, :HALVES] = np.sin(turn)

    def split(table):
        table = table.astype(np.float32)
        high = table.astype(jnp.bfloat16)
        low = (table - high.astype(np.float32)).astype(jnp.bfloat16)
        return [high, low]

    matrices = np.stack(split(forward) + split(inverse))
    return matrices, twiddle.astype(np.float32)


def real_dft(xs):
    n = len(xs)
    if n == 1:
        return [(xs[0], None)]
    even, odd = real_dft(xs[0::2]), real_dft(xs[1::2])
    h = n // 2
    out = [None] * (h + 1)
    out[0] = (even[0][0] + odd[0][0], None)
    out[h] = (even[0][0] - odd[0][0], None)
    for k in range(1, h // 2 + 1):
        if 2 * k == h:
            out[k] = (even[k][0], -odd[k][0])
            continue
        c, s = math.cos(2 * math.pi * k / n), math.sin(2 * math.pi * k / n)
        (er, ei), (orr, oi) = even[k], odd[k]
        tr = orr * c + oi * s
        ti = oi * c - orr * s
        out[k] = (er + tr, ei + ti)
        out[h - k] = (er - tr, ti - ei)
    return out


def real_idft(fs):
    h = len(fs) - 1
    n = 2 * h
    if n == 2:
        return [fs[0][0] + fs[1][0], fs[0][0] - fs[1][0]]
    even, odd = [None] * (h // 2 + 1), [None] * (h // 2 + 1)
    even[0] = (fs[0][0] + fs[h][0], None)
    odd[0] = (fs[0][0] - fs[h][0], None)
    for k in range(1, h // 2 + 1):
        if 2 * k == h:
            even[k] = (2.0 * fs[k][0], None)
            odd[k] = (-2.0 * fs[k][1], None)
            continue
        c, s = math.cos(2 * math.pi * k / n), math.sin(2 * math.pi * k / n)
        (ar, ai), (br, bi) = fs[k], fs[h - k]
        even[k] = (ar + br, ai - bi)
        dr, di = ar - br, ai + bi
        odd[k] = (dr * c - di * s, di * c + dr * s)
    ev, od = real_idft(even), real_idft(odd)
    out = [None] * n
    out[0::2] = ev
    out[1::2] = od
    return out


def split_bf16(x):
    high = x.astype(jnp.bfloat16)
    return high, (x - high.astype(jnp.float32)).astype(jnp.bfloat16)


def dot(a, b):
    return jnp.dot(a, b, preferred_element_type=jnp.float32)


def dot_split(a, b):
    return dot(a[0], b[0]) + (dot(a[1], b[0]) + dot(a[0], b[1]))


def encode(a0, a1):
    diagonal = lax.broadcasted_iota(jnp.int32, a0.shape, 0) == lax.broadcasted_iota(
        jnp.int32, a0.shape, 1
    )

    def one(a):
        largest = jnp.max(jnp.abs(a), axis=1, keepdims=True)
        code = jnp.ceil(jnp.log2(jnp.maximum(largest, 1.2e-38)) * CODE)
        factor = jnp.exp2(code * (-0.5 / CODE)) * ROOT
        return jnp.round(a * factor * factor).astype(jnp.int32), code.astype(jnp.int32)

    q0, c0 = one(a0)
    q1, c1 = one(a1)
    words = (q0 << 16) + q1
    codes = jnp.sum(jnp.where(diagonal, (c0 << 16) + c1, 0), axis=0, keepdims=True)
    return words, codes


def decode(words, codes):
    rows = words.shape[0]
    lane = lax.broadcasted_iota(jnp.int32, (1, 128), 1)
    diagonal = lax.broadcasted_iota(jnp.int32, (rows, 128), 0) == lax.broadcasted_iota(
        jnp.int32, (rows, 128), 1
    )
    c1 = (codes << 16) >> 16
    c0 = (codes - c1) >> 16

    def column(code):
        factor = jnp.exp2(code.astype(jnp.float32) * (0.5 / CODE)) * (1.0 / ROOT)
        factor = jnp.where(lane < COMPS, factor, 0.0)
        return jnp.sum(jnp.where(diagonal, factor, 0.0), axis=1, keepdims=True)

    f0, f1 = column(c0), column(c1)
    low = (words << 16) >> 16
    high = (words - low) >> 16
    return high.astype(jnp.float32) * f0 * f0, low.astype(jnp.float32) * f1 * f1


def kernel(
    mult_hbm,
    base_hbm,
    freq_hbm,
    res_off_hbm,
    leave_off_hbm,
    mats_hbm,
    twid_hbm,
    res_count,
    res_scale,
    leave_count,
    leave_dest,
    leave_scale,
    route_blocks,
    route_num,
    out_hbm,
    near_out,
    in_scr,
    out_scr,
    send_f,
    recv_f,
    send_b,
    recv_b,
    x_scr,
    l_scr,
    y_scr,
    gain_scr,
    base_in,
    base_scr,
    freq_in,
    freq_scr,
    mats,
    twid,
    res_off,
    leave_off,
    pos,
    acc,
    near_tx,
    near_rx,
    in_sem,
    out_sem,
    par_sem,
    fs_sem,
    fr_sem,
    bs_sem,
    br_sem,
    ns_sem,
    nr_sem,
):
    me = lax.axis_index("gz")
    slab = lax.axis_index("gx")
    lower, higher = lax.rem(slab + GX - 1, GX), lax.rem(slab + 1, GX)

    in_copies = [
        pltpu.make_async_copy(
            mult_hbm.at[:, pl.ds(c * 32, 32), :],
            in_scr.reshape(ROWS, CELLS, PLANES).at[pl.ds(0, COMPS), pl.ds(c * 32, 32), :],
            in_sem.at[c],
        )
        for c in range(2)
    ]
    for copy in in_copies:
        copy.start()
    par_copies = [
        pltpu.make_async_copy(src, dst, par_sem.at[i])
        for i, (src, dst) in enumerate(
            [
                (base_hbm, base_in),
                (freq_hbm, freq_in),
                (res_off_hbm, res_off),
                (leave_off_hbm, leave_off),
                (mats_hbm, mats),
                (twid_hbm, twid),
            ]
        )
    ]
    for copy in par_copies:
        copy.start()

    barrier = pltpu.get_barrier_semaphore()

    def greet(s, _):
        pl.semaphore_signal(
            barrier, inc=1, device_id={"gz": lax.rem(me + s, GZ)}, device_id_type=MESH
        )
        return 0

    lax.fori_loop(1, GZ, greet, 0)
    for side in (lower, higher):
        pl.semaphore_signal(barrier, inc=1, device_id={"gx": side}, device_id_type=MESH)

    in_scr[pl.ds(COMPS * CELLS, (ROWS - COMPS) * CELLS), :] = jnp.zeros(
        ((ROWS - COMPS) * CELLS, PLANES), jnp.float32
    )

    def forward_words(c, peer):
        first = c * 32 + 2 * peer
        return encode(
            in_scr[pl.ds(first, ROWS, stride=CELLS), :],
            in_scr[pl.ds(first + 1, ROWS, stride=CELLS), :],
        )

    def copy_f(c, s, sender, receiver):
        return pltpu.make_async_remote_copy(
            src_ref=send_f.at[c, receiver, pl.ds(0, SENT)],
            dst_ref=recv_f.at[c, sender, pl.ds(0, SENT)],
            send_sem=fs_sem.at[c, s],
            recv_sem=fr_sem.at[c, s],
            device_id={"gz": receiver},
            device_id_type=MESH,
        )

    def copy_b(c, s, sender, receiver):
        return pltpu.make_async_remote_copy(
            src_ref=send_b.at[c, receiver, pl.ds(0, SENT)],
            dst_ref=recv_b.at[c, sender, pl.ds(0, SENT)],
            send_sem=bs_sem.at[c, s],
            recv_sem=br_sem.at[c, s],
            device_id={"gz": receiver},
            device_id_type=MESH,
        )

    def put(ref, c, slot, words, codes):
        ref[c, slot, :, :] = words
        ref[c, slot, pl.ds(COMPS, 1), :] = codes

    def peer_after(s):
        return lax.rem(me + s, GZ)

    def peer_before(s):
        return lax.rem(me + GZ - s, GZ)

    def forward_send(c):
        def step(s, _):
            peer = peer_after(s)
            words, codes = forward_words(c, peer)
            put(send_f, c, peer, words, codes)
            copy_f(c, s, me, peer).start()
            return 0

        lax.fori_loop(1, GZ, step, 0)
        words, codes = forward_words(c, me)
        put(recv_f, c, me, words, codes)

    in_copies[0].wait()
    pl.semaphore_wait(barrier, GZ + 1)
    forward_send(0)
    in_copies[1].wait()
    forward_send(1)

    for copy in par_copies:
        copy.wait()
    near_tx[...] = jnp.zeros_like(near_tx)
    lane = lax.broadcasted_iota(jnp.int32, (1, 128), 1)
    for d in range(2):

        def pack(e, _, d=d):
            block = route_blocks[0, 0, d, e]
            scaled = leave_scale[0, 0, block] * leave_off[block].astype(jnp.float32)
            near_tx[d, e, pl.ds(0, 3), :] = scaled.astype(jnp.bfloat16).astype(jnp.float32)
            live = (lane < leave_count[0, 0, block]) & (lane * 0 + e < route_num[0, 0, d])
            near_tx[d, e, pl.ds(3, 1), :] = jnp.where(live, particle_mass, 0.0)
            near_tx[d, e, pl.ds(4, 1), :] = (lane * 0 + leave_dest[0, 0, block]).astype(
                jnp.float32
            )
            return 0

        lax.fori_loop(0, MAXB, pack, 0)

    def copy_n(d):
        return pltpu.make_async_remote_copy(
            src_ref=near_tx.at[d],
            dst_ref=near_rx.at[pl.ds(MAXB * (1 - d), MAXB)],
            send_sem=ns_sem.at[d],
            recv_sem=nr_sem.at[d],
            device_id={"gx": higher if d == 1 else lower},
            device_id_type=MESH,
        )

    for d in range(2):
        copy_n(d).start()

    base_scr[...] = jnp.zeros_like(base_scr)
    base_scr[pl.ds(0, COMPS), pl.ds(0, COMPS)] = base_in[...]
    y_scr[...] = jnp.zeros_like(y_scr)
    freq_scr[...] = jnp.zeros_like(freq_scr)
    freq_scr[pl.ds(0, 1025), pl.ds(0, COMPS)] = freq_in[...]
    for f1 in range(HALVES):
        rows = jnp.concatenate(
            [
                freq_scr[pl.ds(f1, 64, stride=GZ), :],
                freq_scr[pl.ds(GZ - f1, 64, stride=GZ), :],
            ],
            axis=0,
        )
        gain_scr[f1] = jnp.transpose(rows)[0:ROWS] * (1.0 / (GZ * PLANES))

    row3 = lax.broadcasted_iota(jnp.int32, (3, 128), 0)
    sub8 = lax.broadcasted_iota(jnp.int32, (8, 128), 0)
    pos[...] = jnp.zeros_like(pos)
    acc[...] = jnp.zeros_like(acc)

    def place(b, _):
        centre = jnp.where(row3 == 1, b, 0).astype(jnp.float32)
        pos[b + 1, pl.ds(0, 3), :] = (
            res_scale[0, 0, b] * res_off[b].astype(jnp.float32) + centre
        )
        return 0

    lax.fori_loop(0, BLK, place, 0)

    def pull(sinks, source_t, mass_of):
        rows = [[jnp.broadcast_to(p[i : i + 1, :], (8, 128)) for i in range(3)] for p in sinks]
        sums = [[jnp.zeros((8, 128), jnp.float32) for _ in range(3)] for _ in sinks]
        for g in range(16):
            part = source_t[8 * g : 8 * g + 8, :]
            q = [jnp.broadcast_to(part[:, i : i + 1], (8, 128)) for i in range(3)]
            mass = mass_of(g, part)
            for n, p in enumerate(rows):
                d = [q[i] - p[i] for i in range(3)]
                square = d[0] * d[0] + d[1] * d[1] + d[2] * d[2] + softening_sq
                inverse = lax.rsqrt(square)
                weight = mass * inverse * inverse * inverse
                for i in range(3):
                    sums[n][i] = sums[n][i] + d[i] * weight
        return sums

    def resident(b, _):
        count = res_count[0, 0, b]
        source_t = jnp.transpose(pos[b + 1])

        def mass_of(g, part):
            return jnp.where(sub8 + 8 * g < count, particle_mass, 0.0)

        sums = pull([pos[b], pos[b + 1], pos[b + 2]], source_t, mass_of)
        for n in range(3):
            for i in range(3):
                acc[b + n, i] = acc[b + n, i] + sums[n][i]
        return 0

    lax.fori_loop(0, BLK, resident, 0)

    def stack3(sums):
        out = jnp.zeros((8, 128), jnp.float32)
        for i in range(3):
            total = jnp.sum(sums[i], axis=0, keepdims=True)
            out = jnp.where(sub8 == i, jnp.broadcast_to(total, (8, 128)), out)
        return out

    def settle(b, _):
        near_out[b] = stack3([acc[b + 1, i] for i in range(3)])
        return 0

    lax.fori_loop(0, BLK, settle, 0)

    def arrivals():
        for d in range(2):
            copy_n(d).wait()

        def arrival(a, _):
            block = near_rx[a]
            target = jnp.broadcast_to(block[4:5, :], (8, 128))
            sink = jnp.zeros((8, 128), jnp.float32)
            for b in range(BLK):
                sink = sink + jnp.where(target == float(b), pos[b + 1], 0.0)
            source_t = jnp.transpose(block + jnp.where(sub8 == 1, target, 0.0))

            def mass_of(g, part):
                return jnp.broadcast_to(part[:, 3:4], (8, 128))

            pulled = stack3(pull([sink], source_t, mass_of)[0])
            for b in range(BLK):
                near_out[b] = near_out[b] + jnp.where(target == float(b), pulled, 0.0)
            return 0

        lax.fori_loop(0, 2 * MAXB, arrival, 0)

    def open_pencil(c, sender):
        words = recv_f[c, sender]
        a0, a1 = decode(words, recv_f[c, sender, pl.ds(COMPS, 1), :])
        x_scr[0, sender] = a0
        x_scr[1, sender] = a1

    def pencils(c):
        open_pencil(c, me)

        def take(s, _):
            sender = peer_before(s)
            copy_f(c, s, sender, me).wait_recv()
            open_pencil(c, sender)
            return 0

        lax.fori_loop(1, GZ, take, 0)

        def spread(i, _):
            col, tile = i // 11, pl.multiple_of((i % 11) * 8, 8)
            found = real_dft([x_scr[col, d, pl.ds(tile, 8), :] for d in range(GZ)])
            for f1 in range(HALVES):
                re, im = found[f1]
                cos = jnp.broadcast_to(twid[0, f1 : f1 + 1, :], (8, 128))
                sin = jnp.broadcast_to(twid[1, f1 : f1 + 1, :], (8, 128))
                if f1 == 0:
                    out = (re, jnp.zeros_like(re))
                elif im is None:
                    out = (re * cos, -re * sin)
                else:
                    out = (re * cos + im * sin, im * cos - re * sin)
                l_scr[f1, col, pl.ds(tile, 8), pl.ds(0, 128)] = out[0]
                l_scr[f1, col, pl.ds(tile, 8), pl.ds(128, 128)] = out[1]
            return 0

        lax.fori_loop(0, 22, spread, 0)

        def convolve(g, _):
            at = pl.ds(g * 3, 3)
            spec = dot_split(
                split_bf16(l_scr[at].reshape(6 * ROWS, 256)), (mats[0], mats[1])
            ).reshape(3, 2, ROWS, 256)
            gain = gain_scr[at]
            gain = jnp.concatenate([gain, gain], axis=2)[:, None]
            back = dot_split(
                split_bf16((spec * gain).reshape(6 * ROWS, 256)), (mats[2], mats[3])
            )
            l_scr[at] = back.reshape(3, 2, ROWS, 256)
            return 0

        lax.fori_loop(0, 3, convolve, 0)

        def gather(i, _):
            col, tile = i // 11, pl.multiple_of((i % 11) * 8, 8)
            freqs = []
            for f1 in range(HALVES):
                re = l_scr[f1, col, pl.ds(tile, 8), pl.ds(0, 128)]
                if f1 == 0:
                    freqs.append((re, None))
                    continue
                im = l_scr[f1, col, pl.ds(tile, 8), pl.ds(128, 128)]
                cos = jnp.broadcast_to(twid[0, f1 : f1 + 1, :], (8, 128))
                sin = jnp.broadcast_to(twid[1, f1 : f1 + 1, :], (8, 128))
                if f1 == HALVES - 1:
                    freqs.append((re * cos - im * sin, None))
                else:
                    freqs.append((re * cos - im * sin, im * cos + re * sin))
            for d, value in enumerate(real_idft(freqs)):
                y_scr[d, col, pl.ds(tile, 8), :] = value
            return 0

        lax.fori_loop(0, 22, gather, 0)

        base = split_bf16(base_scr[...])

        def mixed_words(d):
            both = jnp.concatenate([y_scr[d, 0], y_scr[d, 1]], axis=1)
            mixed = dot_split(base, split_bf16(both))
            return encode(mixed[:, 0:128], mixed[:, 128:256])

        def answer(s, _):
            peer = peer_after(s)
            words, codes = mixed_words(peer)
            put(send_b, c, peer, words, codes)
            copy_b(c, s, me, peer).start()
            return 0

        lax.fori_loop(1, GZ, answer, 0)
        words, codes = mixed_words(me)
        put(recv_b, c, me, words, codes)

    def close_pencil(c, sender):
        words = recv_b[c, sender]
        a0, a1 = decode(words, recv_b[c, sender, pl.ds(COMPS, 1), :])
        first = c * 32 + 2 * sender
        out_scr[pl.ds(first, ROWS, stride=CELLS), :] = a0
        out_scr[pl.ds(first + 1, ROWS, stride=CELLS), :] = a1

    def out_copy(c):
        return pltpu.make_async_copy(
            out_scr.reshape(ROWS, CELLS, PLANES).at[pl.ds(0, COMPS), pl.ds(c * 32, 32), :],
            out_hbm.at[:, pl.ds(c * 32, 32), :],
            out_sem.at[c],
        )

    def results(c):
        close_pencil(c, me)

        def take(s, _):
            sender = peer_before(s)
            copy_b(c, s, sender, me).wait_recv()
            close_pencil(c, sender)
            return 0

        lax.fori_loop(1, GZ, take, 0)
        out_copy(c).start()

    pencils(0)
    arrivals()
    pencils(1)
    results(0)
    results(1)

    def drain(s, _):
        for c in range(2):
            copy_f(c, s, me, peer_after(s)).wait_send()
            copy_b(c, s, me, peer_after(s)).wait_send()
        return 0

    lax.fori_loop(1, GZ, drain, 0)
    for c in range(2):
        out_copy(c).wait()


def on_device(
    multipoles,
    kernel_base,
    kernel_freq,
    res_off,
    res_count,
    res_scale,
    leave_off,
    leave_count,
    leave_dest,
    leave_scale,
    route_blocks,
    route_num,
):
    matrices, twiddle = dft_tables()
    anywhere = pl.BlockSpec(memory_space=pl.ANY)
    smem = pl.BlockSpec(memory_space=pltpu.SMEM)
    vmem = pl.BlockSpec(memory_space=pltpu.VMEM)
    f32, i32 = jnp.float32, jnp.int32
    dma = pltpu.SemaphoreType.DMA
    taylors, near = pl.pallas_call(
        kernel,
        out_shape=(
            jax.ShapeDtypeStruct((COMPS, CELLS, PLANES), f32),
            jax.ShapeDtypeStruct((BLK, 8, 128), f32),
        ),
        in_specs=[anywhere] * 7 + [smem] * 7,
        out_specs=(anywhere, vmem),
        scratch_shapes=[
            pltpu.VMEM((ROWS * CELLS, PLANES), f32),
            pltpu.VMEM((ROWS * CELLS, PLANES), f32),
            pltpu.VMEM((2, GZ, ROWS, 128), i32),
            pltpu.VMEM((2, GZ, ROWS, 128), i32),
            pltpu.VMEM((2, GZ, ROWS, 128), i32),
            pltpu.VMEM((2, GZ, ROWS, 128), i32),
            pltpu.VMEM((2, GZ, ROWS, 128), f32),
            pltpu.VMEM((HALVES, 2, ROWS, 256), f32),
            pltpu.VMEM((GZ, 2, 128, 128), f32),
            pltpu.VMEM((HALVES, ROWS, 128), f32),
            pltpu.VMEM((COMPS, COMPS), f32),
            pltpu.VMEM((ROWS, 128), f32),
            pltpu.VMEM((1025, COMPS), f32),
            pltpu.VMEM((1040, 128), f32),
            pltpu.VMEM((4, 256, 256), jnp.bfloat16),
            pltpu.VMEM((2, 16, 128), f32),
            pltpu.VMEM((BLK, 3, 128), jnp.bfloat16),
            pltpu.VMEM((POOL, 3, 128), jnp.bfloat16),
            pltpu.VMEM((BLK + 2, 8, 128), f32),
            pltpu.VMEM((BLK + 2, 3, 8, 128), f32),
            pltpu.VMEM((2, MAXB, 8, 128), f32),
            pltpu.VMEM((2 * MAXB, 8, 128), f32),
            dma((2,)),
            dma((2,)),
            dma((6,)),
            dma((2, GZ)),
            dma((2, GZ)),
            dma((2, GZ)),
            dma((2, GZ)),
            dma((2,)),
            dma((2,)),
        ],
        compiler_params=pltpu.CompilerParams(
            collective_id=0, has_side_effects=True, vmem_limit_bytes=48 * 2**20
        ),
    )(
        multipoles.reshape(COMPS, CELLS, PLANES),
        kernel_base,
        kernel_freq,
        res_off[0, 0],
        leave_off[0, 0],
        jnp.asarray(matrices),
        jnp.asarray(twiddle),
        res_count,
        res_scale,
        leave_count,
        leave_dest,
        leave_scale,
        route_blocks,
        route_num,
    )
    return (taylors.reshape(multipoles.shape), near[:, 0:3][None, None])


def solution(mesh):
    in_specs = (
        P(None, "gx", None, "gz"),
        P(),
        P(),
        P("gx", "gz", None, None, None),
        P("gx", "gz", None),
        P("gx", "gz", None),
        P("gx", "gz", None, None, None),
        P("gx", "gz", None),
        P("gx", "gz", None),
        P("gx", "gz", None),
        P("gx", "gz", None, None),
        P("gx", "gz", None),
    )
    out_specs = (P(None, "gx", None, "gz"), P("gx", "gz", None, None, None))
    return jax.shard_map(
        on_device, mesh=mesh, in_specs=in_specs, out_specs=out_specs, check_vma=False
    )
```

```python
import math

import jax
import jax.numpy as jnp
import numpy as np
from jax import lax
from jax.experimental import pallas as pl
from jax.experimental.pallas import tpu as pltpu
from jax.sharding import PartitionSpec as P

softening_sq = 0.04
particle_mass = 1.0 / 128.0
MESH = pl.DeviceIdType.MESH

COMPS = 81
ROWS = 88
SENT = 82
GZ = 16
GX = 32
PLANES = 128
CELLS = 64
HALVES = 9
BLK = 32
POOL = 16
MAXB = 8
TOP = 32700.0
CODE = 128.0
ROOT = math.sqrt(TOP)


def dft_tables():
    r = np.arange(PLANES)
    j = np.arange(PLANES)
    f2 = np.where(j < 64, j, 191 - j)
    angle = 2.0 * np.pi * ((r[:, None] * f2[None, :]) % PLANES) / PLANES
    c, s = np.cos(angle), np.sin(angle)
    forward = np.block([[c, -s], [s, c]])
    inverse = np.block([[c.T, s.T], [-s.T, c.T]])
    turn = 2.0 * np.pi * np.arange(HALVES)[:, None] * r[None, :] / (GZ * PLANES)
    twiddle = np.zeros((2, 16, PLANES))
    twiddle[0, :HALVES] = np.cos(turn)
    twiddle[1, :HALVES] = np.sin(turn)
    return np.stack([forward, inverse]).astype(np.float32), twiddle.astype(np.float32)


def real_dft(xs):
    n = len(xs)
    if n == 1:
        return [(xs[0], None)]
    even, odd = real_dft(xs[0::2]), real_dft(xs[1::2])
    h = n // 2
    out = [None] * (h + 1)
    out[0] = (even[0][0] + odd[0][0], None)
    out[h] = (even[0][0] - odd[0][0], None)
    for k in range(1, h // 2 + 1):
        if 2 * k == h:
            out[k] = (even[k][0], -odd[k][0])
            continue
        c, s = math.cos(2 * math.pi * k / n), math.sin(2 * math.pi * k / n)
        (er, ei), (orr, oi) = even[k], odd[k]
        tr = orr * c + oi * s
        ti = oi * c - orr * s
        out[k] = (er + tr, ei + ti)
        out[h - k] = (er - tr, ti - ei)
    return out


def real_idft(fs):
    h = len(fs) - 1
    n = 2 * h
    if n == 2:
        return [fs[0][0] + fs[1][0], fs[0][0] - fs[1][0]]
    even, odd = [None] * (h // 2 + 1), [None] * (h // 2 + 1)
    even[0] = (fs[0][0] + fs[h][0], None)
    odd[0] = (fs[0][0] - fs[h][0], None)
    for k in range(1, h // 2 + 1):
        if 2 * k == h:
            even[k] = (2.0 * fs[k][0], None)
            odd[k] = (-2.0 * fs[k][1], None)
            continue
        c, s = math.cos(2 * math.pi * k / n), math.sin(2 * math.pi * k / n)
        (ar, ai), (br, bi) = fs[k], fs[h - k]
        even[k] = (ar + br, ai - bi)
        dr, di = ar - br, ai + bi
        odd[k] = (dr * c - di * s, di * c + dr * s)
    ev, od = real_idft(even), real_idft(odd)
    out = [None] * n
    out[0::2] = ev
    out[1::2] = od
    return out


def split_bf16(x):
    high = x.astype(jnp.bfloat16)
    return high, (x - high.astype(jnp.float32)).astype(jnp.bfloat16)


def dot(a, b):
    return jnp.dot(a, b, preferred_element_type=jnp.float32)


def dot_split(a, b):
    return dot(a[0], b[0]) + (dot(a[1], b[0]) + dot(a[0], b[1]))


def encode(a0, a1):
    diagonal = lax.broadcasted_iota(jnp.int32, a0.shape, 0) == lax.broadcasted_iota(
        jnp.int32, a0.shape, 1
    )

    def one(a):
        largest = jnp.max(jnp.abs(a), axis=1, keepdims=True)
        code = jnp.ceil(jnp.log2(jnp.maximum(largest, 1.2e-38)) * CODE)
        factor = jnp.exp2(code * (-0.5 / CODE)) * ROOT
        return jnp.round(a * factor * factor).astype(jnp.int32), code.astype(jnp.int32)

    q0, c0 = one(a0)
    q1, c1 = one(a1)
    words = (q0 << 16) + q1
    codes = jnp.sum(jnp.where(diagonal, (c0 << 16) + c1, 0), axis=0, keepdims=True)
    return words, codes


def decode(words, codes):
    rows = words.shape[0]
    lane = lax.broadcasted_iota(jnp.int32, (1, 128), 1)
    diagonal = lax.broadcasted_iota(jnp.int32, (rows, 128), 0) == lax.broadcasted_iota(
        jnp.int32, (rows, 128), 1
    )
    c1 = (codes << 16) >> 16
    c0 = (codes - c1) >> 16

    def column(code):
        factor = jnp.exp2(code.astype(jnp.float32) * (0.5 / CODE)) * (1.0 / ROOT)
        factor = jnp.where(lane < COMPS, factor, 0.0)
        return jnp.sum(jnp.where(diagonal, factor, 0.0), axis=1, keepdims=True)

    f0, f1 = column(c0), column(c1)
    low = (words << 16) >> 16
    high = (words - low) >> 16
    return high.astype(jnp.float32) * f0 * f0, low.astype(jnp.float32) * f1 * f1


def kernel(
    mult_hbm,
    base_hbm,
    freq_hbm,
    res_off_hbm,
    leave_off_hbm,
    mats_hbm,
    twid_hbm,
    res_count_hbm,
    res_scale_hbm,
    leave_count_hbm,
    leave_dest_hbm,
    leave_scale_hbm,
    route_blocks_hbm,
    route_num_hbm,
    out,
    near_out,
    in_scr,
    send_f,
    recv_f,
    send_b,
    recv_b,
    x_scr,
    l_scr,
    y_scr,
    gain_scr,
    base_in,
    base_scr,
    freq_in,
    freq_scr,
    mats_in,
    mats,
    twid,
    res_off,
    leave_off,
    res_count,
    res_scale,
    leave_count,
    leave_dest,
    leave_scale,
    route_blocks,
    route_num,
    leave_rows,
    pos_rows,
    acc,
    near,
    near_tx,
    near_rx,
    in_sem,
    par_sem,
    fs_sem,
    fr_sem,
    bs_sem,
    br_sem,
    ns_sem,
    nr_sem,
):
    me = lax.axis_index("gz")
    slab = lax.axis_index("gx")
    lower, higher = lax.rem(slab + GX - 1, GX), lax.rem(slab + 1, GX)

    in_copies = [
        pltpu.make_async_copy(
            mult_hbm.at[:, pl.ds(c * 32, 32), :],
            in_scr.reshape(ROWS, CELLS, PLANES).at[pl.ds(0, COMPS), pl.ds(c * 32, 32), :],
            in_sem.at[c],
        )
        for c in range(2)
    ]
    for copy in in_copies:
        copy.start()
    barrier = pltpu.get_barrier_semaphore()

    def greet(s, _):
        pl.semaphore_signal(
            barrier, inc=1, device_id={"gz": lax.rem(me + s, GZ)}, device_id_type=MESH
        )
        return 0

    lax.fori_loop(1, GZ, greet, 0)
    for side in (lower, higher):
        pl.semaphore_signal(barrier, inc=1, device_id={"gx": side}, device_id_type=MESH)

    par_copies = [
        pltpu.make_async_copy(src, dst, par_sem.at[i])
        for i, (src, dst) in enumerate(
            [
                (base_hbm, base_in),
                (freq_hbm, freq_in),
                (res_off_hbm, res_off),
                (leave_off_hbm, leave_off),
                (mats_hbm, mats_in),
                (twid_hbm, twid),
                (res_count_hbm, res_count),
                (res_scale_hbm, res_scale),
                (leave_count_hbm, leave_count),
                (leave_dest_hbm, leave_dest),
                (leave_scale_hbm, leave_scale),
                (route_blocks_hbm, route_blocks),
                (route_num_hbm, route_num),
            ]
        )
    ]
    for copy in par_copies:
        copy.start()

    in_scr[pl.ds(COMPS * CELLS, (ROWS - COMPS) * CELLS), :] = jnp.zeros(
        ((ROWS - COMPS) * CELLS, PLANES), jnp.float32
    )

    def forward_words(c, peer):
        first = c * 32 + 2 * peer
        return encode(
            in_scr[pl.ds(first, ROWS, stride=CELLS), :],
            in_scr[pl.ds(first + 1, ROWS, stride=CELLS), :],
        )

    def copy_f(c, s, sender, receiver):
        return pltpu.make_async_remote_copy(
            src_ref=send_f.at[c, receiver, pl.ds(0, SENT)],
            dst_ref=recv_f.at[c, sender, pl.ds(0, SENT)],
            send_sem=fs_sem.at[c, s],
            recv_sem=fr_sem.at[c, s],
            device_id={"gz": receiver},
            device_id_type=MESH,
        )

    def copy_b(c, s, sender, receiver):
        return pltpu.make_async_remote_copy(
            src_ref=send_b.at[c, receiver, pl.ds(0, SENT)],
            dst_ref=recv_b.at[c, sender, pl.ds(0, SENT)],
            send_sem=bs_sem.at[c, s],
            recv_sem=br_sem.at[c, s],
            device_id={"gz": receiver},
            device_id_type=MESH,
        )

    def put(ref, c, slot, words, codes):
        ref[c, slot, :, :] = words
        ref[c, slot, pl.ds(COMPS, 1), :] = codes

    def peer_after(s):
        return lax.rem(me + s, GZ)

    def peer_before(s):
        return lax.rem(me + GZ - s, GZ)

    def forward_send(c):
        def step(s, _):
            peer = peer_after(s)
            words, codes = forward_words(c, peer)
            put(send_f, c, peer, words, codes)
            copy_f(c, s, me, peer).start()
            return 0

        lax.fori_loop(1, GZ, step, 0)
        words, codes = forward_words(c, me)
        put(recv_f, c, me, words, codes)

    in_copies[0].wait()
    pl.semaphore_wait(barrier, GZ + 1)
    forward_send(0)
    in_copies[1].wait()
    forward_send(1)

    for copy in par_copies:
        copy.wait()
    near_tx[...] = jnp.zeros_like(near_tx)
    for i in range(3):
        leave_rows.reshape(POOL * 8, 128)[pl.ds(i, POOL, stride=8), :] = leave_off[i].astype(
            jnp.float32
        )
    lane = lax.broadcasted_iota(jnp.int32, (1, 128), 1)
    for d in range(2):

        def pack(e, _, d=d):
            block = route_blocks[0, 0, d, e]
            scaled = leave_scale[0, 0, block] * leave_rows[block][0:3]
            near_tx[d, e, pl.ds(0, 3), :] = scaled.astype(jnp.bfloat16).astype(jnp.float32)
            live = (lane < leave_count[0, 0, block]) & (lane * 0 + e < route_num[0, 0, d])
            near_tx[d, e, pl.ds(3, 1), :] = jnp.where(live, particle_mass, 0.0)
            near_tx[d, e, pl.ds(4, 1), :] = (lane * 0 + leave_dest[0, 0, block]).astype(
                jnp.float32
            )
            return 0

        lax.fori_loop(0, MAXB, pack, 0)

    def copy_n(d):
        return pltpu.make_async_remote_copy(
            src_ref=near_tx.at[d],
            dst_ref=near_rx.at[pl.ds(MAXB * (1 - d), MAXB)],
            send_sem=ns_sem.at[d],
            recv_sem=nr_sem.at[d],
            device_id={"gx": higher if d == 1 else lower},
            device_id_type=MESH,
        )

    for d in range(2):
        copy_n(d).start()

    for i in range(2):
        mats[2 * i], mats[2 * i + 1] = split_bf16(mats_in[i])
    base_scr[...] = jnp.zeros_like(base_scr)
    base_scr[pl.ds(0, COMPS), pl.ds(0, COMPS)] = base_in[...]
    y_scr[...] = jnp.zeros_like(y_scr)
    freq_scr[...] = jnp.zeros_like(freq_scr)
    for i in range(8):
        part = freq_in[:, i * 128 : i * 128 + 128]
        part = jnp.concatenate([part, jnp.zeros((128 - COMPS, 128), jnp.float32)], axis=0)
        freq_scr[pl.ds(i * 128, 128), :] = jnp.transpose(part)
    last = jnp.broadcast_to(freq_in[:, 1024:1025], (COMPS, 128))
    last = jnp.concatenate([last, jnp.zeros((128 - COMPS, 128), jnp.float32)], axis=0)
    freq_scr[pl.ds(1024, 1), :] = jnp.transpose(last)[0:1]
    for f1 in range(HALVES):
        rows = jnp.concatenate(
            [
                freq_scr[pl.ds(f1, 64, stride=GZ), :],
                freq_scr[pl.ds(GZ - f1, 64, stride=GZ), :],
            ],
            axis=0,
        )
        gain_scr[f1] = jnp.transpose(rows)[0:ROWS] * (1.0 / (GZ * PLANES))

    sub8 = lax.broadcasted_iota(jnp.int32, (8, 128), 0)
    pos_rows[...] = jnp.zeros_like(pos_rows)
    pos = pos_rows.reshape(BLK + 2, 8, 128)
    acc[...] = jnp.zeros_like(acc)
    for i in range(3):
        pos_rows[pl.ds(8 + i, BLK, stride=8), :] = res_off[i].astype(jnp.float32)

    def place(b, _):
        centre = jnp.where(sub8 == 1, b, 0).astype(jnp.float32)
        pos[b + 1] = res_scale[0, 0, b] * pos[b + 1] + centre
        return 0

    lax.fori_loop(0, BLK, place, 0)

    def pull(sinks, source_t, mass_of):
        rows = [[jnp.broadcast_to(p[i : i + 1, :], (8, 128)) for i in range(3)] for p in sinks]
        sums = [[jnp.zeros((8, 128), jnp.float32) for _ in range(3)] for _ in sinks]
        for g in range(16):
            part = source_t[8 * g : 8 * g + 8, :]
            q = [jnp.broadcast_to(part[:, i : i + 1], (8, 128)) for i in range(3)]
            mass = mass_of(g, part)
            for n, p in enumerate(rows):
                d = [q[i] - p[i] for i in range(3)]
                square = d[0] * d[0] + d[1] * d[1] + d[2] * d[2] + softening_sq
                inverse = lax.rsqrt(square)
                weight = mass * inverse * inverse * inverse
                for i in range(3):
                    sums[n][i] = sums[n][i] + d[i] * weight
        return sums

    def resident(b, _):
        count = res_count[0, 0, b]
        source_t = jnp.transpose(pos[b + 1])

        def mass_of(g, part):
            return jnp.where(sub8 + 8 * g < count, particle_mass, 0.0)

        sums = pull([pos[b], pos[b + 1], pos[b + 2]], source_t, mass_of)
        for n in range(3):
            for i in range(3):
                acc[b + n, i] = acc[b + n, i] + sums[n][i]
        return 0

    lax.fori_loop(0, BLK, resident, 0)

    def stack3(sums):
        out = jnp.zeros((8, 128), jnp.float32)
        for i in range(3):
            total = jnp.sum(sums[i], axis=0, keepdims=True)
            out = jnp.where(sub8 == i, jnp.broadcast_to(total, (8, 128)), out)
        return out

    def settle(b, _):
        near[pl.ds(pl.multiple_of(b * 8, 8), 8), :] = stack3([acc[b + 1, i] for i in range(3)])
        return 0

    lax.fori_loop(0, BLK, settle, 0)

    def arrivals():
        for d in range(2):
            copy_n(d).wait()

        def arrival(a, _):
            block = near_rx[a]
            target = jnp.broadcast_to(block[4:5, :], (8, 128))
            sink = jnp.zeros((8, 128), jnp.float32)
            for b in range(BLK):
                sink = sink + jnp.where(target == float(b), pos[b + 1], 0.0)
            source_t = jnp.transpose(block + jnp.where(sub8 == 1, target, 0.0))

            def mass_of(g, part):
                return jnp.broadcast_to(part[:, 3:4], (8, 128))

            pulled = stack3(pull([sink], source_t, mass_of)[0])
            for b in range(BLK):
                at = pl.ds(b * 8, 8)
                near[at, :] = near[at, :] + jnp.where(target == float(b), pulled, 0.0)
            return 0

        lax.fori_loop(0, 2 * MAXB, arrival, 0)
        for i in range(3):
            near_out[i] = near[pl.ds(i, BLK, stride=8), :]

    def open_pencil(c, sender):
        words = recv_f[c, sender]
        a0, a1 = decode(words, recv_f[c, sender, pl.ds(COMPS, 1), :])
        x_scr[0, sender] = a0
        x_scr[1, sender] = a1

    def pencils(c):
        open_pencil(c, me)

        def take(s, _):
            sender = peer_before(s)
            copy_f(c, s, sender, me).wait_recv()
            open_pencil(c, sender)
            return 0

        lax.fori_loop(1, GZ, take, 0)

        def spread(i, _):
            col, tile = i // 11, pl.multiple_of((i % 11) * 8, 8)
            found = real_dft([x_scr[col, d, pl.ds(tile, 8), :] for d in range(GZ)])
            for f1 in range(HALVES):
                re, im = found[f1]
                cos = jnp.broadcast_to(twid[0, f1 : f1 + 1, :], (8, 128))
                sin = jnp.broadcast_to(twid[1, f1 : f1 + 1, :], (8, 128))
                if f1 == 0:
                    out = (re, jnp.zeros_like(re))
                elif im is None:
                    out = (re * cos, -re * sin)
                else:
                    out = (re * cos + im * sin, im * cos - re * sin)
                l_scr[f1, col, pl.ds(tile, 8), pl.ds(0, 128)] = out[0]
                l_scr[f1, col, pl.ds(tile, 8), pl.ds(128, 128)] = out[1]
            return 0

        lax.fori_loop(0, 22, spread, 0)

        def convolve(g, _):
            at = pl.ds(g * 3, 3)
            spec = dot_split(
                split_bf16(l_scr[at].reshape(6 * ROWS, 256)), (mats[0], mats[1])
            ).reshape(3, 2, ROWS, 256)
            gain = gain_scr[at]
            gain = jnp.concatenate([gain, gain], axis=2)[:, None]
            back = dot_split(
                split_bf16((spec * gain).reshape(6 * ROWS, 256)), (mats[2], mats[3])
            )
            l_scr[at] = back.reshape(3, 2, ROWS, 256)
            return 0

        lax.fori_loop(0, 3, convolve, 0)

        def gather(i, _):
            col, tile = i // 11, pl.multiple_of((i % 11) * 8, 8)
            freqs = []
            for f1 in range(HALVES):
                re = l_scr[f1, col, pl.ds(tile, 8), pl.ds(0, 128)]
                if f1 == 0:
                    freqs.append((re, None))
                    continue
                im = l_scr[f1, col, pl.ds(tile, 8), pl.ds(128, 128)]
                cos = jnp.broadcast_to(twid[0, f1 : f1 + 1, :], (8, 128))
                sin = jnp.broadcast_to(twid[1, f1 : f1 + 1, :], (8, 128))
                if f1 == HALVES - 1:
                    freqs.append((re * cos - im * sin, None))
                else:
                    freqs.append((re * cos - im * sin, im * cos + re * sin))
            for d, value in enumerate(real_idft(freqs)):
                y_scr[d, col, pl.ds(tile, 8), :] = value
            return 0

        lax.fori_loop(0, 22, gather, 0)

        base = split_bf16(base_scr[...])

        def mixed_words(d):
            both = jnp.concatenate([y_scr[d, 0], y_scr[d, 1]], axis=1)
            mixed = dot_split(base, split_bf16(both))
            return encode(mixed[:, 0:128], mixed[:, 128:256])

        def answer(s, _):
            peer = peer_after(s)
            words, codes = mixed_words(peer)
            put(send_b, c, peer, words, codes)
            copy_b(c, s, me, peer).start()
            return 0

        lax.fori_loop(1, GZ, answer, 0)
        words, codes = mixed_words(me)
        put(recv_b, c, me, words, codes)

    def close_pencil(c, sender):
        words = recv_b[c, sender]
        a0, a1 = decode(words, recv_b[c, sender, pl.ds(COMPS, 1), :])
        first = c * 32 + 2 * sender
        out[pl.ds(first, COMPS, stride=CELLS), :] = a0[0:COMPS]
        out[pl.ds(first + 1, COMPS, stride=CELLS), :] = a1[0:COMPS]

    def results(c):
        close_pencil(c, me)

        def take(s, _):
            sender = peer_before(s)
            copy_b(c, s, sender, me).wait_recv()
            close_pencil(c, sender)
            return 0

        lax.fori_loop(1, GZ, take, 0)

    pencils(0)
    arrivals()
    pencils(1)
    results(0)
    results(1)

    def drain(s, _):
        for c in range(2):
            copy_f(c, s, me, peer_after(s)).wait_send()
            copy_b(c, s, me, peer_after(s)).wait_send()
        return 0

    lax.fori_loop(1, GZ, drain, 0)


def write_out(far, near, far_hbm, near_hbm, sem):
    copies = [pltpu.make_async_copy(near, near_hbm, sem.at[9])]
    size = COMPS * CELLS // 9
    for i in range(9):
        part = pl.ds(i * size, size)
        copies.append(pltpu.make_async_copy(far.at[part], far_hbm.at[part], sem.at[i]))
    for copy in copies:
        copy.start()
    for copy in copies:
        copy.wait()


def on_device(
    multipoles,
    kernel_base,
    kernel_freq,
    res_off,
    res_count,
    res_scale,
    leave_off,
    leave_count,
    leave_dest,
    leave_scale,
    route_blocks,
    route_num,
):
    matrices, twiddle = dft_tables()
    hbm = pl.BlockSpec(memory_space=pltpu.HBM)
    vmem = pl.BlockSpec(memory_space=pltpu.VMEM)
    f32, i32 = jnp.float32, jnp.int32
    dma = pltpu.SemaphoreType.DMA
    operands = [
        multipoles.reshape(COMPS, CELLS, PLANES),
        kernel_base,
        jnp.transpose(kernel_freq),
        jnp.transpose(res_off[0, 0], (1, 0, 2)),
        jnp.transpose(leave_off[0, 0], (1, 0, 2)),
        jnp.asarray(matrices),
        jnp.asarray(twiddle),
        res_count,
        res_scale,
        leave_count,
        leave_dest,
        leave_scale,
        route_blocks,
        route_num,
    ]
    operands = [pltpu.with_memory_space_constraint(x, pltpu.HBM) for x in operands]
    taylors, near = pl.pallas_call(
        kernel,
        out_shape=(
            pltpu.VMEM((COMPS * CELLS, PLANES), f32),
            pltpu.VMEM((3, BLK, 128), f32),
        ),
        in_specs=[hbm] * 14,
        out_specs=(vmem, vmem),
        scratch_shapes=[
            pltpu.VMEM((ROWS * CELLS, PLANES), f32),
            pltpu.VMEM((2, GZ, ROWS, 128), i32),
            pltpu.VMEM((2, GZ, ROWS, 128), i32),
            pltpu.VMEM((2, GZ, ROWS, 128), i32),
            pltpu.VMEM((2, GZ, ROWS, 128), i32),
            pltpu.VMEM((2, GZ, ROWS, 128), f32),
            pltpu.VMEM((HALVES, 2, ROWS, 256), f32),
            pltpu.VMEM((GZ, 2, 128, 128), f32),
            pltpu.VMEM((HALVES, ROWS, 128), f32),
            pltpu.VMEM((COMPS, COMPS), f32),
            pltpu.VMEM((ROWS, 128), f32),
            pltpu.VMEM((COMPS, 1025), f32),
            pltpu.VMEM((1040, 128), f32),
            pltpu.VMEM((2, 256, 256), f32),
            pltpu.VMEM((4, 256, 256), jnp.bfloat16),
            pltpu.VMEM((2, 16, 128), f32),
            pltpu.VMEM((3, BLK, 128), jnp.bfloat16),
            pltpu.VMEM((3, POOL, 128), jnp.bfloat16),
            pltpu.SMEM((1, 1, BLK), i32),
            pltpu.SMEM((1, 1, BLK), f32),
            pltpu.SMEM((1, 1, POOL), i32),
            pltpu.SMEM((1, 1, POOL), i32),
            pltpu.SMEM((1, 1, POOL), f32),
            pltpu.SMEM((1, 1, 2, MAXB), i32),
            pltpu.SMEM((1, 1, 2), i32),
            pltpu.VMEM((POOL, 8, 128), f32),
            pltpu.VMEM(((BLK + 2) * 8, 128), f32),
            pltpu.VMEM((BLK + 2, 3, 8, 128), f32),
            pltpu.VMEM((BLK * 8, 128), f32),
            pltpu.VMEM((2, MAXB, 8, 128), f32),
            pltpu.VMEM((2 * MAXB, 8, 128), f32),
            dma((2,)),
            dma((13,)),
            dma((2, GZ)),
            dma((2, GZ)),
            dma((2, GZ)),
            dma((2, GZ)),
            dma((2,)),
            dma((2,)),
        ],
        compiler_params=pltpu.CompilerParams(
            collective_id=0, has_side_effects=True, vmem_limit_bytes=40 * 2**20
        ),
    )(*operands)
    taylors, near = pl.pallas_call(
        write_out,
        out_shape=(
            pltpu.HBM((COMPS * CELLS, PLANES), f32),
            pltpu.HBM((3, BLK, 128), f32),
        ),
        in_specs=[vmem] * 2,
        out_specs=(hbm, hbm),
        scratch_shapes=[dma((10,))],
    )(*[pltpu.with_memory_space_constraint(x, pltpu.VMEM) for x in (taylors, near)])
    return (taylors.reshape(multipoles.shape), jnp.transpose(near, (1, 0, 2))[None, None])


def solution(mesh):
    in_specs = (
        P(None, "gx", None, "gz"),
        P(),
        P(),
        P("gx", "gz", None, None, None),
        P("gx", "gz", None),
        P("gx", "gz", None),
        P("gx", "gz", None, None, None),
        P("gx", "gz", None),
        P("gx", "gz", None),
        P("gx", "gz", None),
        P("gx", "gz", None, None),
        P("gx", "gz", None),
    )
    out_specs = (P(None, "gx", None, "gz"), P("gx", "gz", None, None, None))
    return jax.shard_map(
        on_device, mesh=mesh, in_specs=in_specs, out_specs=out_specs, check_vma=False
    )
```

```python
import math

import jax
import jax.numpy as jnp
import numpy as np
from jax import lax
from jax.experimental import pallas as pl
from jax.experimental.pallas import tpu as pltpu
from jax.sharding import PartitionSpec as P

softening_sq = 0.04
particle_mass = 1.0 / 128.0
MESH = pl.DeviceIdType.MESH

COMPS = 81
ROWS = 88
SENT = 82
GZ = 16
GX = 32
PLANES = 128
CELLS = 64
HALVES = 9
BLK = 32
POOL = 16
MAXB = 8
TOP = 32700.0
CODE = 128.0
ROOT = math.sqrt(TOP)


def dft_tables():
    r = np.arange(PLANES)
    j = np.arange(PLANES)
    f2 = np.where(j < 64, j, 191 - j)
    angle = 2.0 * np.pi * ((r[:, None] * f2[None, :]) % PLANES) / PLANES
    c, s = np.cos(angle), np.sin(angle)
    forward = np.block([[c, -s], [s, c]])
    inverse = np.block([[c.T, s.T], [-s.T, c.T]])
    turn = 2.0 * np.pi * np.arange(HALVES)[:, None] * r[None, :] / (GZ * PLANES)
    twiddle = np.zeros((2, 16, PLANES))
    twiddle[0, :HALVES] = np.cos(turn)
    twiddle[1, :HALVES] = np.sin(turn)
    return np.stack([forward, inverse]).astype(np.float32), twiddle.astype(np.float32)


def real_dft(xs):
    n = len(xs)
    if n == 1:
        return [(xs[0], None)]
    even, odd = real_dft(xs[0::2]), real_dft(xs[1::2])
    h = n // 2
    out = [None] * (h + 1)
    out[0] = (even[0][0] + odd[0][0], None)
    out[h] = (even[0][0] - odd[0][0], None)
    for k in range(1, h // 2 + 1):
        if 2 * k == h:
            out[k] = (even[k][0], -odd[k][0])
            continue
        c, s = math.cos(2 * math.pi * k / n), math.sin(2 * math.pi * k / n)
        (er, ei), (orr, oi) = even[k], odd[k]
        tr = orr * c + oi * s
        ti = oi * c - orr * s
        out[k] = (er + tr, ei + ti)
        out[h - k] = (er - tr, ti - ei)
    return out


def real_idft(fs):
    h = len(fs) - 1
    n = 2 * h
    if n == 2:
        return [fs[0][0] + fs[1][0], fs[0][0] - fs[1][0]]
    even, odd = [None] * (h // 2 + 1), [None] * (h // 2 + 1)
    even[0] = (fs[0][0] + fs[h][0], None)
    odd[0] = (fs[0][0] - fs[h][0], None)
    for k in range(1, h // 2 + 1):
        if 2 * k == h:
            even[k] = (2.0 * fs[k][0], None)
            odd[k] = (-2.0 * fs[k][1], None)
            continue
        c, s = math.cos(2 * math.pi * k / n), math.sin(2 * math.pi * k / n)
        (ar, ai), (br, bi) = fs[k], fs[h - k]
        even[k] = (ar + br, ai - bi)
        dr, di = ar - br, ai + bi
        odd[k] = (dr * c - di * s, di * c + dr * s)
    ev, od = real_idft(even), real_idft(odd)
    out = [None] * n
    out[0::2] = ev
    out[1::2] = od
    return out


def split_bf16(x):
    high = x.astype(jnp.bfloat16)
    return high, (x - high.astype(jnp.float32)).astype(jnp.bfloat16)


def dot(a, b):
    return jnp.dot(a, b, preferred_element_type=jnp.float32)


def dot_split(a, b):
    return dot(a[0], b[0]) + (dot(a[1], b[0]) + dot(a[0], b[1]))


def encode(a0, a1):
    diagonal = lax.broadcasted_iota(jnp.int32, a0.shape, 0) == lax.broadcasted_iota(
        jnp.int32, a0.shape, 1
    )

    def one(a):
        largest = jnp.max(jnp.abs(a), axis=1, keepdims=True)
        code = jnp.ceil(jnp.log2(jnp.maximum(largest, 1.2e-38)) * CODE)
        factor = jnp.exp2(code * (-0.5 / CODE)) * ROOT
        return jnp.round(a * factor * factor).astype(jnp.int32), code.astype(jnp.int32)

    q0, c0 = one(a0)
    q1, c1 = one(a1)
    words = (q0 << 16) + q1
    codes = jnp.sum(jnp.where(diagonal, (c0 << 16) + c1, 0), axis=0, keepdims=True)
    return words, codes


def decode(words, codes):
    rows = words.shape[0]
    lane = lax.broadcasted_iota(jnp.int32, (1, 128), 1)
    first = lax.broadcasted_iota(jnp.int32, (8, 128), 0) == 0
    c1 = (codes << 16) >> 16
    c0 = (codes - c1) >> 16

    def factor(code):
        found = jnp.exp2(code.astype(jnp.float32) * (0.5 / CODE)) * (1.0 / ROOT)
        return jnp.broadcast_to(jnp.where(lane < COMPS, found, 0.0), (8, 128))

    factors = jnp.transpose(jnp.where(first, factor(c0), factor(c1)))
    f0, f1 = factors[0:rows, 0:1], factors[0:rows, 1:2]
    low = (words << 16) >> 16
    high = (words - low) >> 16
    return high.astype(jnp.float32) * f0 * f0, low.astype(jnp.float32) * f1 * f1


def kernel(
    mult_hbm,
    base_hbm,
    freq_hbm,
    res_off_hbm,
    leave_off_hbm,
    mats_hbm,
    twid_hbm,
    res_count_hbm,
    res_scale_hbm,
    leave_count_hbm,
    leave_dest_hbm,
    leave_scale_hbm,
    route_blocks_hbm,
    route_num_hbm,
    out,
    near_out,
    in_scr,
    send_f,
    recv_f,
    send_b,
    recv_b,
    x_scr,
    l_scr,
    y_scr,
    gain_scr,
    base_in,
    base_scr,
    freq_in,
    freq_scr,
    mats_in,
    mats,
    twid,
    res_off,
    leave_off,
    res_count,
    res_scale,
    leave_count,
    leave_dest,
    leave_scale,
    route_blocks,
    route_num,
    leave_rows,
    pos_rows,
    acc,
    near,
    near_tx,
    near_rx,
    in_sem,
    par_sem,
    fs_sem,
    fr_sem,
    bs_sem,
    br_sem,
    ns_sem,
    nr_sem,
):
    me = lax.axis_index("gz")
    slab = lax.axis_index("gx")
    lower, higher = lax.rem(slab + GX - 1, GX), lax.rem(slab + 1, GX)

    barrier = pltpu.get_barrier_semaphore()

    def greet(s, _):
        pl.semaphore_signal(
            barrier, inc=1, device_id={"gz": lax.rem(me + s, GZ)}, device_id_type=MESH
        )
        return 0

    lax.fori_loop(1, GZ, greet, 0)
    for side in (lower, higher):
        pl.semaphore_signal(barrier, inc=1, device_id={"gx": side}, device_id_type=MESH)

    in_copies = [
        pltpu.make_async_copy(
            mult_hbm.at[:, pl.ds(c * 32, 32), :],
            in_scr.reshape(ROWS + 1, CELLS, PLANES).at[pl.ds(0, COMPS), pl.ds(c * 32, 32), :],
            in_sem.at[c],
        )
        for c in range(2)
    ]
    for copy in in_copies:
        copy.start()
    par_copies = [
        pltpu.make_async_copy(src, dst, par_sem.at[i])
        for i, (src, dst) in enumerate(
            [
                (base_hbm, base_in),
                (freq_hbm, freq_in),
                (res_off_hbm, res_off),
                (leave_off_hbm, leave_off),
                (mats_hbm, mats_in),
                (twid_hbm, twid),
                (res_count_hbm, res_count),
                (res_scale_hbm, res_scale),
                (leave_count_hbm, leave_count),
                (leave_dest_hbm, leave_dest),
                (leave_scale_hbm, leave_scale),
                (route_blocks_hbm, route_blocks),
                (route_num_hbm, route_num),
            ]
        )
    ]
    for copy in par_copies:
        copy.start()

    in_scr[pl.ds(COMPS * CELLS, (ROWS + 1 - COMPS) * CELLS), :] = jnp.zeros(
        ((ROWS + 1 - COMPS) * CELLS, PLANES), jnp.float32
    )

    def forward_words(c, peer):
        first = c * 32 + 2 * peer
        return encode(
            in_scr[pl.ds(first, ROWS, stride=CELLS), :],
            in_scr[pl.ds(first + 1, ROWS, stride=CELLS), :],
        )

    def copy_f(c, s, sender, receiver):
        return pltpu.make_async_remote_copy(
            src_ref=send_f.at[c, receiver, pl.ds(0, SENT)],
            dst_ref=recv_f.at[c, sender, pl.ds(0, SENT)],
            send_sem=fs_sem.at[c, s],
            recv_sem=fr_sem.at[c, s],
            device_id={"gz": receiver},
            device_id_type=MESH,
        )

    def copy_b(c, sender, receiver):
        return pltpu.make_async_remote_copy(
            src_ref=send_b.at[c, receiver, pl.ds(0, SENT)],
            dst_ref=recv_b.at[c, sender, pl.ds(0, SENT)],
            send_sem=bs_sem.at[c, receiver],
            recv_sem=br_sem.at[c, sender],
            device_id={"gz": receiver},
            device_id_type=MESH,
        )

    def put(ref, c, slot, words, codes):
        ref[c, slot, :, :] = words
        ref[c, slot, pl.ds(COMPS, 1), :] = codes

    def peer_after(s):
        return lax.rem(me + s, GZ)

    def peer_before(s):
        return lax.rem(me + GZ - s, GZ)

    def forward_send(c):
        def step(s, _):
            peer = peer_after(s)
            words, codes = forward_words(c, peer)
            put(send_f, c, peer, words, codes)
            copy_f(c, s, me, peer).start()
            return 0

        lax.fori_loop(1, GZ, step, 0)
        words, codes = forward_words(c, me)
        put(recv_f, c, me, words, codes)

    in_copies[0].wait()
    pl.semaphore_wait(barrier, GZ + 1)
    forward_send(0)
    in_copies[1].wait()
    forward_send(1)

    for copy in par_copies:
        copy.wait()
    near_tx[...] = jnp.zeros_like(near_tx)
    for i in range(3):
        leave_rows.reshape((POOL + 1) * 8, 128)[pl.ds(i, POOL, stride=8), :] = leave_off[i].astype(
            jnp.float32
        )
    lane = lax.broadcasted_iota(jnp.int32, (1, 128), 1)
    for d in range(2):

        def pack(e, _, d=d):
            block = route_blocks[0, 0, d, e]
            scaled = leave_scale[0, 0, block] * leave_rows[block][0:3]
            near_tx[d, e, pl.ds(0, 3), :] = scaled.astype(jnp.bfloat16).astype(jnp.float32)
            live = (lane < leave_count[0, 0, block]) & (lane * 0 + e < route_num[0, 0, d])
            near_tx[d, e, pl.ds(3, 1), :] = jnp.where(live, particle_mass, 0.0)
            near_tx[d, e, pl.ds(4, 1), :] = (lane * 0 + leave_dest[0, 0, block]).astype(
                jnp.float32
            )
            return 0

        lax.fori_loop(0, MAXB, pack, 0)

    def copy_n(d):
        return pltpu.make_async_remote_copy(
            src_ref=near_tx.at[d],
            dst_ref=near_rx.at[pl.ds(MAXB * (1 - d), MAXB)],
            send_sem=ns_sem.at[d],
            recv_sem=nr_sem.at[d],
            device_id={"gx": higher if d == 1 else lower},
            device_id_type=MESH,
        )

    for d in range(2):
        copy_n(d).start()

    for i in range(2):
        mats[2 * i], mats[2 * i + 1] = split_bf16(mats_in[i])
    base_scr[...] = jnp.zeros_like(base_scr)
    base_scr[pl.ds(0, COMPS), pl.ds(0, COMPS)] = base_in[...]
    y_scr[...] = jnp.zeros_like(y_scr)
    freq_scr[...] = jnp.zeros_like(freq_scr)
    for i in range(8):
        part = freq_in[:, i * 128 : i * 128 + 128]
        part = jnp.concatenate([part, jnp.zeros((128 - COMPS, 128), jnp.float32)], axis=0)
        freq_scr[pl.ds(i * 128, 128), :] = jnp.transpose(part)
    last = jnp.broadcast_to(freq_in[:, 1024:1025], (COMPS, 128))
    last = jnp.concatenate([last, jnp.zeros((128 - COMPS, 128), jnp.float32)], axis=0)
    freq_scr[pl.ds(1024, 1), :] = jnp.transpose(last)[0:1]
    for f1 in range(HALVES):
        rows = jnp.concatenate(
            [
                freq_scr[pl.ds(f1, 64, stride=GZ), :],
                freq_scr[pl.ds(GZ - f1, 64, stride=GZ), :],
            ],
            axis=0,
        )
        gain_scr[f1] = jnp.transpose(rows)[0:ROWS] * (1.0 / (GZ * PLANES))

    sub8 = lax.broadcasted_iota(jnp.int32, (8, 128), 0)
    pos_rows[...] = jnp.zeros_like(pos_rows)
    pos = pos_rows.reshape(BLK + 2, 8, 128)
    acc[...] = jnp.zeros_like(acc)
    for i in range(3):
        pos_rows[pl.ds(8 + i, BLK, stride=8), :] = res_off[i].astype(jnp.float32)

    def place(b, _):
        centre = jnp.where(sub8 == 1, b, 0).astype(jnp.float32)
        pos[b + 1] = res_scale[0, 0, b] * pos[b + 1] + centre
        return 0

    lax.fori_loop(0, BLK, place, 0)

    def pull(sinks, source_t, mass_of):
        rows = [[jnp.broadcast_to(p[i : i + 1, :], (8, 128)) for i in range(3)] for p in sinks]
        sums = [[jnp.zeros((8, 128), jnp.float32) for _ in range(3)] for _ in sinks]
        for g in range(16):
            part = source_t[8 * g : 8 * g + 8, :]
            q = [jnp.broadcast_to(part[:, i : i + 1], (8, 128)) for i in range(3)]
            mass = mass_of(g, part)
            for n, p in enumerate(rows):
                d = [q[i] - p[i] for i in range(3)]
                square = d[0] * d[0] + d[1] * d[1] + d[2] * d[2] + softening_sq
                inverse = lax.rsqrt(square)
                weight = mass * inverse * inverse * inverse
                for i in range(3):
                    sums[n][i] = sums[n][i] + d[i] * weight
        return sums

    def resident(b, _):
        count = res_count[0, 0, b]
        source_t = jnp.transpose(pos[b + 1])

        def mass_of(g, part):
            return jnp.where(sub8 + 8 * g < count, particle_mass, 0.0)

        sums = pull([pos[b], pos[b + 1], pos[b + 2]], source_t, mass_of)
        for n in range(3):
            for i in range(3):
                acc[b + n, i] = acc[b + n, i] + sums[n][i]
        return 0

    lax.fori_loop(0, BLK, resident, 0)

    def stack3(sums):
        out = jnp.zeros((8, 128), jnp.float32)
        for i in range(3):
            total = jnp.sum(sums[i], axis=0, keepdims=True)
            out = jnp.where(sub8 == i, jnp.broadcast_to(total, (8, 128)), out)
        return out

    def settle(b, _):
        near[pl.ds(pl.multiple_of(b * 8, 8), 8), :] = stack3([acc[b + 1, i] for i in range(3)])
        return 0

    lax.fori_loop(0, BLK, settle, 0)

    def arrivals():
        for d in range(2):
            copy_n(d).wait()

        def arrival(a, _):
            block = near_rx[a]
            target = jnp.broadcast_to(block[4:5, :], (8, 128))
            sink = jnp.zeros((8, 128), jnp.float32)
            for b in range(BLK):
                sink = sink + jnp.where(target == float(b), pos[b + 1], 0.0)
            source_t = jnp.transpose(block + jnp.where(sub8 == 1, target, 0.0))

            def mass_of(g, part):
                return jnp.broadcast_to(part[:, 3:4], (8, 128))

            pulled = stack3(pull([sink], source_t, mass_of)[0])
            for b in range(BLK):
                at = pl.ds(b * 8, 8)
                near[at, :] = near[at, :] + jnp.where(target == float(b), pulled, 0.0)
            return 0

        lax.fori_loop(0, 2 * MAXB, arrival, 0)
        for i in range(3):
            near_out[i] = near[pl.ds(i, BLK, stride=8), :]

    def open_pencil(c, sender):
        words = recv_f[c, sender]
        a0, a1 = decode(words, recv_f[c, sender, pl.ds(COMPS, 1), :])
        x_scr[0, sender] = a0
        x_scr[1, sender] = a1

    def pencils(c):
        open_pencil(c, me)

        def take(s, _):
            sender = peer_before(s)
            copy_f(c, s, sender, me).wait_recv()
            open_pencil(c, sender)
            return 0

        lax.fori_loop(1, GZ, take, 0)

        def spread(i, _):
            col, tile = i // 11, pl.multiple_of((i % 11) * 8, 8)
            found = real_dft([x_scr[col, d, pl.ds(tile, 8), :] for d in range(GZ)])
            for f1 in range(HALVES):
                re, im = found[f1]
                cos = jnp.broadcast_to(twid[0, f1 : f1 + 1, :], (8, 128))
                sin = jnp.broadcast_to(twid[1, f1 : f1 + 1, :], (8, 128))
                if f1 == 0:
                    out = (re, jnp.zeros_like(re))
                elif im is None:
                    out = (re * cos, -re * sin)
                else:
                    out = (re * cos + im * sin, im * cos - re * sin)
                l_scr[f1, col, pl.ds(tile, 8), pl.ds(0, 128)] = out[0]
                l_scr[f1, col, pl.ds(tile, 8), pl.ds(128, 128)] = out[1]
            return 0

        lax.fori_loop(0, 22, spread, 0)

        def convolve(g, _):
            at = pl.ds(g * 3, 3)
            spec = dot_split(
                split_bf16(l_scr[at].reshape(6 * ROWS, 256)), (mats[0], mats[1])
            ).reshape(3, 2, ROWS, 256)
            gain = gain_scr[at]
            gain = jnp.concatenate([gain, gain], axis=2)[:, None]
            back = dot_split(
                split_bf16((spec * gain).reshape(6 * ROWS, 256)), (mats[2], mats[3])
            )
            l_scr[at] = back.reshape(3, 2, ROWS, 256)
            return 0

        lax.fori_loop(0, 3, convolve, 0)

        def gather(i, _):
            col, tile = i // 11, pl.multiple_of((i % 11) * 8, 8)
            freqs = []
            for f1 in range(HALVES):
                re = l_scr[f1, col, pl.ds(tile, 8), pl.ds(0, 128)]
                if f1 == 0:
                    freqs.append((re, None))
                    continue
                im = l_scr[f1, col, pl.ds(tile, 8), pl.ds(128, 128)]
                cos = jnp.broadcast_to(twid[0, f1 : f1 + 1, :], (8, 128))
                sin = jnp.broadcast_to(twid[1, f1 : f1 + 1, :], (8, 128))
                if f1 == HALVES - 1:
                    freqs.append((re * cos - im * sin, None))
                else:
                    freqs.append((re * cos - im * sin, im * cos + re * sin))
            for d, value in enumerate(real_idft(freqs)):
                y_scr[d, col, pl.ds(tile, 8), :] = value
            return 0

        lax.fori_loop(0, 22, gather, 0)

        base = split_bf16(base_scr[...])

        def mixed_words(d):
            both = jnp.concatenate([y_scr[d, 0], y_scr[d, 1]], axis=1)
            mixed = dot_split(base, split_bf16(both))
            return encode(mixed[:, 0:128], mixed[:, 128:256])

        def answer(s, _):
            peer = peer_after(s + 1)
            words, codes = mixed_words(peer)

            @pl.when(peer == me)
            def _():
                put(recv_b, c, me, words, codes)

            @pl.when(peer != me)
            def _():
                put(send_b, c, peer, words, codes)
                copy_b(c, me, peer).start()

            return 0

        lax.fori_loop(0, GZ, answer, 0)

    def close_pencil(c, sender):
        words = recv_b[c, sender]
        a0, a1 = decode(words, recv_b[c, sender, pl.ds(COMPS, 1), :])
        first = c * 32 + 2 * sender
        out[pl.ds(first, COMPS, stride=CELLS), :] = a0[0:COMPS]
        out[pl.ds(first + 1, COMPS, stride=CELLS), :] = a1[0:COMPS]

    def results(c):
        close_pencil(c, me)

        def take(s, _):
            sender = peer_before(s)
            copy_b(c, sender, me).wait_recv()
            close_pencil(c, sender)
            return 0

        lax.fori_loop(1, GZ, take, 0)

    pencils(0)
    arrivals()
    pencils(1)
    results(0)
    results(1)

    def drain(s, _):
        for c in range(2):
            copy_f(c, s, me, peer_after(s)).wait_send()
            copy_b(c, me, peer_after(s)).wait_send()
        return 0

    lax.fori_loop(1, GZ, drain, 0)


def write_out(far, near, far_hbm, near_hbm, sem):
    copies = [pltpu.make_async_copy(near, near_hbm, sem.at[9])]
    size = COMPS * CELLS // 9
    for i in range(9):
        part = pl.ds(i * size, size)
        copies.append(pltpu.make_async_copy(far.at[part], far_hbm.at[part], sem.at[i]))
    for copy in copies:
        copy.start()
    for copy in copies:
        copy.wait()


def on_device(
    multipoles,
    kernel_base,
    kernel_freq,
    res_off,
    res_count,
    res_scale,
    leave_off,
    leave_count,
    leave_dest,
    leave_scale,
    route_blocks,
    route_num,
):
    matrices, twiddle = dft_tables()
    hbm = pl.BlockSpec(memory_space=pltpu.HBM)
    vmem = pl.BlockSpec(memory_space=pltpu.VMEM)
    f32, i32 = jnp.float32, jnp.int32
    dma = pltpu.SemaphoreType.DMA
    operands = [
        multipoles.reshape(COMPS, CELLS, PLANES),
        kernel_base,
        jnp.transpose(kernel_freq),
        jnp.transpose(res_off[0, 0], (1, 0, 2)),
        jnp.transpose(leave_off[0, 0], (1, 0, 2)),
        jnp.asarray(matrices),
        jnp.asarray(twiddle),
        res_count,
        res_scale,
        leave_count,
        leave_dest,
        leave_scale,
        route_blocks,
        route_num,
    ]
    operands = [pltpu.with_memory_space_constraint(x, pltpu.HBM) for x in operands]
    taylors, near = pl.pallas_call(
        kernel,
        out_shape=(
            pltpu.VMEM(((COMPS + 1) * CELLS, PLANES), f32),
            pltpu.VMEM((3, BLK, 128), f32),
        ),
        in_specs=[hbm] * 14,
        out_specs=(vmem, vmem),
        scratch_shapes=[
            pltpu.VMEM(((ROWS + 1) * CELLS, PLANES), f32),
            pltpu.VMEM((2, GZ, ROWS, 128), i32),
            pltpu.VMEM((2, GZ, ROWS, 128), i32),
            pltpu.VMEM((2, GZ, ROWS, 128), i32),
            pltpu.VMEM((2, GZ, ROWS, 128), i32),
            pltpu.VMEM((2, GZ, ROWS, 128), f32),
            pltpu.VMEM((HALVES, 2, ROWS, 256), f32),
            pltpu.VMEM((GZ, 2, 128, 128), f32),
            pltpu.VMEM((HALVES, ROWS, 128), f32),
            pltpu.VMEM((COMPS, COMPS), f32),
            pltpu.VMEM((ROWS, 128), f32),
            pltpu.VMEM((COMPS, 1025), f32),
            pltpu.VMEM((1040, 128), f32),
            pltpu.VMEM((2, 256, 256), f32),
            pltpu.VMEM((4, 256, 256), jnp.bfloat16),
            pltpu.VMEM((2, 16, 128), f32),
            pltpu.VMEM((3, BLK, 128), jnp.bfloat16),
            pltpu.VMEM((3, POOL, 128), jnp.bfloat16),
            pltpu.SMEM((1, 1, BLK), i32),
            pltpu.SMEM((1, 1, BLK), f32),
            pltpu.SMEM((1, 1, POOL), i32),
            pltpu.SMEM((1, 1, POOL), i32),
            pltpu.SMEM((1, 1, POOL), f32),
            pltpu.SMEM((1, 1, 2, MAXB), i32),
            pltpu.SMEM((1, 1, 2), i32),
            pltpu.VMEM((POOL + 1, 8, 128), f32),
            pltpu.VMEM(((BLK + 2) * 8, 128), f32),
            pltpu.VMEM((BLK + 2, 3, 8, 128), f32),
            pltpu.VMEM(((BLK + 1) * 8, 128), f32),
            pltpu.VMEM((2, MAXB, 8, 128), f32),
            pltpu.VMEM((2 * MAXB, 8, 128), f32),
            dma((2,)),
            dma((13,)),
            dma((2, GZ)),
            dma((2, GZ)),
            dma((2, GZ)),
            dma((2, GZ)),
            dma((2,)),
            dma((2,)),
        ],
        compiler_params=pltpu.CompilerParams(
            collective_id=0, has_side_effects=True, vmem_limit_bytes=40 * 2**20
        ),
    )(*operands)
    taylors, near = pl.pallas_call(
        write_out,
        out_shape=(
            pltpu.HBM((COMPS * CELLS, PLANES), f32),
            pltpu.HBM((3, BLK, 128), f32),
        ),
        in_specs=[vmem] * 2,
        out_specs=(hbm, hbm),
        scratch_shapes=[dma((10,))],
    )(*[pltpu.with_memory_space_constraint(x, pltpu.VMEM) for x in (taylors, near)])
    return (taylors.reshape(multipoles.shape), jnp.transpose(near, (1, 0, 2))[None, None])


def solution(mesh):
    in_specs = (
        P(None, "gx", None, "gz"),
        P(),
        P(),
        P("gx", "gz", None, None, None),
        P("gx", "gz", None),
        P("gx", "gz", None),
        P("gx", "gz", None, None, None),
        P("gx", "gz", None),
        P("gx", "gz", None),
        P("gx", "gz", None),
        P("gx", "gz", None, None),
        P("gx", "gz", None),
    )
    out_specs = (P(None, "gx", None, "gz"), P("gx", "gz", None, None, None))
    return jax.shard_map(
        on_device, mesh=mesh, in_specs=in_specs, out_specs=out_specs, check_vma=False
    )
```
